1024 devices in a mesh: row: 32 (over x, z_hi, core), col: 32 (over z_lo, y).
Axes of the slice: x: 4, y: 8, z: 16 (z_hi: 4, z_lo: 4; z = z_hi * 4 + z_lo), core: 2. Of those that a mesh axis runs over, the one named last changes fastest.
Arguments:
- inputs: bfloat16 [512, 12288], P(None, 'row'), may hold values from -6 to 6
- cotangent: bfloat16 [512, 12288], P(None, 'row'), may hold values from -6 to 6
- w_in: bfloat16 [12288, 24576], P('row', 'col'), may hold values from -0.0546875 to 0.0546875
- w_out: bfloat16 [24576, 12288], P('col', 'row'), may hold values from -0.0390625 to 0.0390625
Outputs:
- mlp_out: float32 [512, 12288], P('col', 'row')
- input_grad: float32 [512, 12288], P('col', 'row')
- w_in_grad: float32 [12288, 24576], P('row', 'col')
- w_out_grad: float32 [24576, 12288], P('col', 'row')
The draws below stay inside these ranges and needn't reach their ends.
All inputs are finite; a program needn't handle non-finite values.
Results may differ from the reference program's by a relative error of at most 0.0029.
Values may be sent and summed in bfloat16 or wider, within the bound.
No kernel may reach another device: no remote copies, remote signals or barrier semaphores. Data moves between devices by JAX's collectives and lax.ppermute only.
A program may use at most 32 MiB of HBM per device.

```python
import jax
import jax.numpy as jnp
from jax import lax

D = 12288
FF = 24576
TOKENS = 512


def level_of(stream_key, shape, pieces, least, largest):
    loudness = 1.0
    for dim, parts in pieces:
        draws = jax.random.uniform(jax.random.fold_in(jax.random.fold_in(stream_key, 6), dim), (parts,), jnp.float32, least / len(pieces), largest / len(pieces))
        loudness = loudness * jnp.repeat(jnp.exp(draws), shape[dim] // parts).reshape((-1,) + (1,) * (len(shape) - 1 - dim))
    return loudness


def normal_values(key, shape, spread, most, split=(), dtype=jnp.bfloat16):
    drawn = spread * jax.random.normal(key, shape, jnp.float32)
    if split:
        drawn = drawn * level_of(key, shape, split, -0.22, 0.18)
    return jnp.clip(drawn, -most, most).astype(dtype)


def setup_inputs(seed: int = 0) -> dict:
    key_of = jax.random.split(jax.random.key(seed), 5)
    return {
        "inputs": normal_values(key_of[0], (TOKENS, D), 1.0, 6.0, ((1, 32),)),
        "cotangent": normal_values(key_of[1], (TOKENS, D), 1.0, 6.0, ((1, 32),)),
        "w_in": normal_values(key_of[2], (D, FF), D ** -0.5, 0.0546875, ((0, 32), (1, 32))),
        "w_out": normal_values(key_of[3], (FF, D), FF ** -0.5, 0.0390625, ((0, 32), (1, 32))),
    }


inv_root_two = 0.7071067811865476
density_scale = 0.3989422804014327


def gelu_value(pre):
    return pre * 0.5 * (1.0 + lax.erf(pre * inv_root_two))


def gelu_slope(pre):
    return 0.5 * (1.0 + lax.erf(pre * inv_root_two)) + pre * density_scale * jnp.exp(-0.5 * pre * pre)


def reference(inputs, cotangent, w_in, w_out):
    pre = jnp.dot(inputs, w_in, preferred_element_type=jnp.float32)
    act = gelu_value(pre).astype(jnp.bfloat16)
    mlp_out = jnp.dot(act, w_out, preferred_element_type=jnp.float32)
    act_grad = jnp.dot(cotangent, w_out.T, preferred_element_type=jnp.float32)
    pre_grad = (act_grad * gelu_slope(pre)).astype(jnp.bfloat16)
    w_out_grad = jnp.dot(act.T, cotangent, preferred_element_type=jnp.float32)
    w_in_grad = jnp.dot(inputs.T, pre_grad, preferred_element_type=jnp.float32)
    input_grad = jnp.dot(pre_grad, w_in.T, preferred_element_type=jnp.float32)
    return (mlp_out, input_grad, w_in_grad, w_out_grad)
```

```python
import jax
import jax.numpy as jnp
from jax import lax
from jax.sharding import Mesh, PartitionSpec as P

inv_root_two = 0.7071067811865476
density_scale = 0.3989422804014327

root_scale = 512.0
smallest = 1e-37


def gelu_value(pre):
    return pre * 0.5 * (1.0 + lax.erf(pre * inv_root_two))


def gelu_slope(pre):
    return 0.5 * (1.0 + lax.erf(pre * inv_root_two)) + pre * density_scale * jnp.exp(
        -0.5 * pre * pre
    )


def to_root(value):
    root = value * lax.rsqrt(jnp.maximum(jnp.abs(value), smallest))
    return (root * root_scale).astype(jnp.float16)


def from_root(root):
    root = root.astype(jnp.float32) * (1.0 / root_scale)
    return root * jnp.abs(root)


def contract_last(left, right):
    return lax.dot_general(
        left, right, (((1,), (1,)), ((), ())), preferred_element_type=jnp.float32
    )


def contract_first(left, right):
    return lax.dot_general(
        left, right, (((0,), (0,)), ((), ())), preferred_element_type=jnp.float32
    )


def exchange(value, axis):
    pieces = lax.all_to_all(value, axis, 0, 0, tiled=True)
    return pieces.reshape(lax.axis_size(axis), -1, value.shape[-1])


def swap_core(value):
    return lax.ppermute(value, "core", [(0, 1), (1, 0)])


def shards(inputs, cotangent, w_in, w_out):
    total, features = inputs.shape
    hidden = w_in.shape[1]
    half = total // 2
    core = lax.axis_index("core")
    zl, ny = lax.axis_size("zl"), lax.axis_size("y")

    def reorder(array):
        return array.reshape(zl, ny, -1, features).transpose(1, 0, 2, 3).reshape(total, features)

    inputs, cotangent = reorder(inputs), reorder(cotangent)
    in_mine = lax.dynamic_slice(inputs, (core * half, 0), (half, features))
    in_other = lax.dynamic_slice(inputs, ((1 - core) * half, 0), (half, features))
    ct_mine = lax.dynamic_slice(cotangent, (core * half, 0), (half, features))
    ct_other = lax.dynamic_slice(cotangent, ((1 - core) * half, 0), (half, features))

    pre_sent = swap_core(jnp.dot(in_other, w_in, preferred_element_type=jnp.float32))
    grad_sent = swap_core(contract_last(ct_other, w_out))
    pre = jnp.dot(in_mine, w_in, preferred_element_type=jnp.float32) + pre_sent
    grad = contract_last(ct_mine, w_out) + grad_sent

    both = jnp.concatenate([to_root(pre), to_root(grad)], axis=1)
    both = to_root(jnp.sum(from_root(exchange(both, "x")), axis=0))
    both = jnp.sum(from_root(exchange(both, "zh")), axis=0)
    pre, grad = both[:, :hidden], both[:, hidden:]
    act = gelu_value(pre).astype(jnp.bfloat16)
    pre_grad = (grad * gelu_slope(pre)).astype(jnp.bfloat16)
    mine = jnp.concatenate([act, pre_grad], axis=1)
    mine = lax.all_gather(mine, "zh", axis=0, tiled=True)
    mine = lax.all_gather(mine, "x", axis=0, tiled=True)
    other = swap_core(mine)
    low = jnp.where(core == 0, mine, other)
    high = jnp.where(core == 0, other, mine)
    act = jnp.concatenate([low[:, :hidden], high[:, :hidden]], axis=0)
    pre_grad = jnp.concatenate([low[:, hidden:], high[:, hidden:]], axis=0)

    out = jnp.dot(act, w_out, preferred_element_type=jnp.float32)
    back = contract_last(pre_grad, w_in)
    sums = jnp.concatenate([out.astype(jnp.bfloat16), back.astype(jnp.bfloat16)], axis=1)
    sums = jnp.sum(exchange(sums, "y").astype(jnp.float32), axis=0)
    sums = jnp.sum(exchange(sums, "zl"), axis=0)
    w_out_grad = contract_first(act, cotangent)
    w_in_grad = contract_first(inputs, pre_grad)
    return (sums[:, :features], sums[:, features:], w_in_grad, w_out_grad)


def solution(mesh):
    fine = Mesh(mesh.devices.reshape(4, 4, 2, 4, 8), ("x", "zh", "core", "zl", "y"))
    row, col = ("x", "zh", "core"), ("zl", "y")
    in_specs = (P(None, row), P(None, row), P(row, col), P(col, row))
    out_specs = (P(col, row), P(col, row), P(row, col), P(col, row))
    return jax.shard_map(shards, mesh=fine, in_specs=in_specs, out_specs=out_specs, check_vma=False)
```

```python
import jax
import jax.numpy as jnp
from jax import lax
from jax.sharding import Mesh, PartitionSpec as P

inv_root_two = 0.7071067811865476
density_scale = 0.3989422804014327

root_scale = 512.0
smallest = 1e-37

fourth_scale = 2048.0


def gelu_value(pre):
    return pre * 0.5 * (1.0 + lax.erf(pre * inv_root_two))


def gelu_slope(pre):
    return 0.5 * (1.0 + lax.erf(pre * inv_root_two)) + pre * density_scale * jnp.exp(
        -0.5 * pre * pre
    )


def to_root(value):
    root = value * lax.rsqrt(jnp.maximum(jnp.abs(value), smallest))
    return (root * root_scale).astype(jnp.float16)


def from_root(root):
    root = root.astype(jnp.float32) * (1.0 / root_scale)
    return root * jnp.abs(root)


def to_fourth_root(value):
    size = jnp.maximum(jnp.abs(value), smallest)
    square = size * lax.rsqrt(size)
    root = square * lax.rsqrt(square) * fourth_scale
    return jnp.where(value < 0.0, -root, root).astype(jnp.float16)


def from_fourth_root(root):
    root = root.astype(jnp.float32) * (1.0 / fourth_scale)
    return root * jnp.abs(root) * (root * root)


def contract_last(left, right):
    return lax.dot_general(
        left, right, (((1,), (1,)), ((), ())), preferred_element_type=jnp.float32
    )


def contract_first(left, right):
    return lax.dot_general(
        left, right, (((0,), (0,)), ((), ())), preferred_element_type=jnp.float32
    )


def exchange(value, axis):
    pieces = lax.all_to_all(value, axis, 0, 0, tiled=True)
    return pieces.reshape(lax.axis_size(axis), -1, value.shape[-1])


def swap_core(value):
    return lax.ppermute(value, "core", [(0, 1), (1, 0)])


def shards(inputs, cotangent, w_in, w_out):
    total, features = inputs.shape
    hidden = w_in.shape[1]
    half = total // 2
    core = lax.axis_index("core")

    def reorder(array):
        blocks = array.reshape(2, 2, 4, 2, -1, features)
        return blocks.transpose(1, 3, 0, 2, 4, 5).reshape(total, features)

    inputs, cotangent = reorder(inputs), reorder(cotangent)
    in_mine = lax.dynamic_slice(inputs, (core * half, 0), (half, features))
    in_other = lax.dynamic_slice(inputs, ((1 - core) * half, 0), (half, features))
    ct_mine = lax.dynamic_slice(cotangent, (core * half, 0), (half, features))
    ct_other = lax.dynamic_slice(cotangent, ((1 - core) * half, 0), (half, features))

    pre_sent = swap_core(jnp.dot(in_other, w_in, preferred_element_type=jnp.float32))
    grad_sent = swap_core(contract_last(ct_other, w_out))
    pre = jnp.dot(in_mine, w_in, preferred_element_type=jnp.float32) + pre_sent
    grad = contract_last(ct_mine, w_out) + grad_sent

    both = jnp.concatenate([to_root(pre), to_root(grad)], axis=1)
    both = to_root(jnp.sum(from_root(exchange(both, "x")), axis=0))
    both = jnp.sum(from_root(exchange(both, "zh")), axis=0)
    pre, grad = both[:, :hidden], both[:, hidden:]
    act = gelu_value(pre).astype(jnp.bfloat16)
    pre_grad = (grad * gelu_slope(pre)).astype(jnp.bfloat16)
    mine = jnp.concatenate([act, pre_grad], axis=1)
    mine = lax.all_gather(mine, "zh", axis=0, tiled=True)
    mine = lax.all_gather(mine, "x", axis=0, tiled=True)
    other = swap_core(mine)
    low = jnp.where(core == 0, mine, other)
    high = jnp.where(core == 0, other, mine)
    act = jnp.concatenate([low[:, :hidden], high[:, :hidden]], axis=0)
    pre_grad = jnp.concatenate([low[:, hidden:], high[:, hidden:]], axis=0)

    out = jnp.dot(act, w_out, preferred_element_type=jnp.float32)
    back = contract_last(pre_grad, w_in)
    sums = jnp.concatenate([out.astype(jnp.bfloat16), back.astype(jnp.bfloat16)], axis=1)
    sums = jnp.sum(exchange(sums, ("zb", "yb")).astype(jnp.float32), axis=0)
    sums = exchange(to_fourth_root(sums), ("za", "ya"))
    sums = jnp.sum(from_fourth_root(sums), axis=0)
    w_out_grad = contract_first(act, cotangent)
    w_in_grad = contract_first(inputs, pre_grad)
    return (sums[:, :features], sums[:, features:], w_in_grad, w_out_grad)


def solution(mesh):
    axes = ("x", "zh", "core", "za", "zb", "ya", "yb")
    fine = Mesh(mesh.devices.reshape(4, 4, 2, 2, 2, 4, 2), axes)
    row, col = axes[:3], axes[3:]
    in_specs = (P(None, row), P(None, row), P(row, col), P(col, row))
    out_specs = (P(col, row), P(col, row), P(row, col), P(col, row))
    return jax.shard_map(shards, mesh=fine, in_specs=in_specs, out_specs=out_specs, check_vma=False)
```

```python
import jax
import jax.numpy as jnp
from jax import lax
from jax.sharding import Mesh, PartitionSpec as P

inv_root_two = 0.7071067811865476
density_scale = 0.3989422804014327

root_scale = 512.0
smallest = 1e-37

fourth_scale = 2048.0


def gelu_value(pre):
    return pre * 0.5 * (1.0 + lax.erf(pre * inv_root_two))


def gelu_slope(pre):
    return 0.5 * (1.0 + lax.erf(pre * inv_root_two)) + pre * density_scale * jnp.exp(
        -0.5 * pre * pre
    )


def signed_root(value):
    return value * lax.rsqrt(jnp.maximum(jnp.abs(value), smallest))


def signed_square(root):
    return root * jnp.abs(root)


def to_root(value):
    return (signed_root(value) * root_scale).astype(jnp.float16)


def from_root(root):
    return signed_square(root.astype(jnp.float32) * (1.0 / root_scale))


def to_fourth_root(value):
    return (signed_root(signed_root(value)) * fourth_scale).astype(jnp.float16)


def from_fourth_root(root):
    return signed_square(signed_square(root.astype(jnp.float32) * (1.0 / fourth_scale)))


def contract_last(left, right):
    return lax.dot_general(
        left, right, (((1,), (1,)), ((), ())), preferred_element_type=jnp.float32
    )


def contract_first(left, right):
    return lax.dot_general(
        left, right, (((0,), (0,)), ((), ())), preferred_element_type=jnp.float32
    )


def exchange(value, axis):
    pieces = lax.all_to_all(value, axis, 0, 0, tiled=True)
    return pieces.reshape(lax.axis_size(axis), -1, value.shape[-1])


def swap_core(value):
    return lax.ppermute(value, "core", [(0, 1), (1, 0)])


def core_order(mine, other, axis):
    first = lax.axis_index("core") == 0
    return jnp.concatenate([jnp.where(first, mine, other), jnp.where(first, other, mine)], axis=axis)


def shards(inputs, cotangent, w_in, w_out):
    total, features = inputs.shape
    hidden = w_in.shape[1]
    half = total // 2
    core = lax.axis_index("core")

    in_mine = lax.dynamic_slice(inputs, (core * half, 0), (half, features))
    in_other = lax.dynamic_slice(inputs, ((1 - core) * half, 0), (half, features))
    ct_mine = lax.dynamic_slice(cotangent, (core * half, 0), (half, features))
    ct_other = lax.dynamic_slice(cotangent, ((1 - core) * half, 0), (half, features))

    pre_sent = swap_core(jnp.dot(in_other, w_in, preferred_element_type=jnp.float32))
    grad_sent = swap_core(contract_last(ct_other, w_out))
    pre = jnp.dot(in_mine, w_in, preferred_element_type=jnp.float32) + pre_sent
    grad = contract_last(ct_mine, w_out) + grad_sent

    both = jnp.concatenate([to_root(pre), to_root(grad)], axis=1)
    both = jnp.sum(from_root(exchange(both, "x")), axis=0)
    both, w_in_late, w_out_late = lax.optimization_barrier((both, w_in, w_out))
    both = exchange(to_root(both), "zh")
    w_in_all = core_order(w_in_late, swap_core(w_in_late), 0)
    w_out_all = core_order(w_out_late, swap_core(w_out_late), 1)
    both = jnp.sum(from_root(both), axis=0)
    pre, grad = both[:, :hidden], both[:, hidden:]
    act = gelu_value(pre).astype(jnp.bfloat16)
    pre_grad = (grad * gelu_slope(pre)).astype(jnp.bfloat16)
    mine = jnp.concatenate([act, pre_grad], axis=1)
    mine = lax.all_gather(mine, "zh", axis=0, tiled=True)
    mine = lax.all_gather(mine, "x", axis=0, tiled=True)

    out = jnp.dot(mine[:, :hidden], w_out_all, preferred_element_type=jnp.float32).astype(jnp.bfloat16)
    back = contract_last(mine[:, hidden:], w_in_all).astype(jnp.bfloat16)
    sums = jnp.concatenate([out[:, :features], back[:, :features]], axis=1)
    sums_next = jnp.concatenate([out[:, features:], back[:, features:]], axis=1)
    sums = jnp.concatenate([sums, sums_next], axis=0).reshape(2, 2, 4, 2, -1, 2 * features)
    sums = sums.transpose(0, 1, 3, 2, 4, 5).reshape(-1, 2 * features)
    sums = exchange(sums, ("core", "zb", "yb"))
    sums = jnp.sum(sums.reshape(2, 4, -1, 2 * features).astype(jnp.float32), axis=1)
    sums = to_fourth_root(sums.reshape(-1, 2 * features))
    sums, mine = lax.optimization_barrier((sums, mine))
    sums = jnp.sum(from_fourth_root(exchange(sums, ("za", "ya"))), axis=0)
    every = core_order(mine, swap_core(mine), 0)
    w_out_grad = contract_first(every[:, :hidden], cotangent)
    w_in_grad = contract_first(inputs, every[:, hidden:])
    return (sums[:, :features], sums[:, features:], w_in_grad, w_out_grad)


def solution(mesh):
    axes = ("x", "zh", "core", "za", "zb", "ya", "yb")
    fine = Mesh(mesh.devices.reshape(4, 4, 2, 2, 2, 4, 2), axes)
    row, col = axes[:3], axes[3:]
    in_specs = (P(None, row), P(None, row), P(row, col), P(col, row))
    out_specs = (P(col, row), P(col, row), P(row, col), P(col, row))
    return jax.shard_map(shards, mesh=fine, in_specs=in_specs, out_specs=out_specs, check_vma=False)
```

```python
import jax
import jax.numpy as jnp
from jax import lax
from jax.sharding import Mesh, PartitionSpec as P

inv_root_two = 0.7071067811865476
density_scale = 0.3989422804014327

root_scale = 512.0
smallest = 1e-37

fourth_scale = 2048.0


def gelu_value(pre):
    return pre * 0.5 * (1.0 + lax.erf(pre * inv_root_two))


def gelu_slope(pre):
    return 0.5 * (1.0 + lax.erf(pre * inv_root_two)) + pre * density_scale * jnp.exp(
        -0.5 * pre * pre
    )


def signed_root(value):
    return value * lax.rsqrt(jnp.maximum(jnp.abs(value), smallest))


def signed_square(root):
    return root * jnp.abs(root)


def to_root(value):
    return (signed_root(value) * root_scale).astype(jnp.float16)


def from_root(root):
    return signed_square(root.astype(jnp.float32) * (1.0 / root_scale))


def to_fourth_root(value):
    return (signed_root(signed_root(value)) * fourth_scale).astype(jnp.float16)


def from_fourth_root(root):
    return signed_square(signed_square(root.astype(jnp.float32) * (1.0 / fourth_scale)))


def contract_last(left, right):
    return lax.dot_general(
        left, right, (((1,), (1,)), ((), ())), preferred_element_type=jnp.float32
    )


def contract_first(left, right):
    return lax.dot_general(
        left, right, (((0,), (0,)), ((), ())), preferred_element_type=jnp.float32
    )


def exchange(value, axis):
    pieces = lax.all_to_all(value, axis, 0, 0, tiled=True)
    return pieces.reshape(lax.axis_size(axis), -1, value.shape[-1])


def swap_core(value):
    return lax.ppermute(value, "core", [(0, 1), (1, 0)])


def core_order(mine, other, axis):
    first = lax.axis_index("core") == 0
    return jnp.concatenate([jnp.where(first, mine, other), jnp.where(first, other, mine)], axis=axis)


def shards(inputs, cotangent, w_in, w_out):
    total, features = inputs.shape
    hidden = w_in.shape[1]
    half = total // 2
    core = lax.axis_index("core")

    in_mine = lax.dynamic_slice(inputs, (core * half, 0), (half, features))
    in_other = lax.dynamic_slice(inputs, ((1 - core) * half, 0), (half, features))
    ct_mine = lax.dynamic_slice(cotangent, (core * half, 0), (half, features))
    ct_other = lax.dynamic_slice(cotangent, ((1 - core) * half, 0), (half, features))

    pre_sent = swap_core(jnp.dot(in_other, w_in, preferred_element_type=jnp.float32))
    grad_sent = swap_core(contract_last(ct_other, w_out))
    pre = jnp.dot(in_mine, w_in, preferred_element_type=jnp.float32) + pre_sent
    grad = contract_last(ct_mine, w_out) + grad_sent

    both = jnp.concatenate([to_root(pre), to_root(grad)], axis=1)
    both = jnp.sum(from_root(exchange(both, "x")), axis=0)
    both, w_in_late, w_out_late = lax.optimization_barrier((both, w_in, w_out))
    both = exchange(to_root(both), "zh")
    w_in_all = core_order(w_in_late, swap_core(w_in_late), 0)
    w_out_all = core_order(w_out_late, swap_core(w_out_late), 1)
    both = jnp.sum(from_root(both), axis=0)
    pre, grad = both[:, :hidden], both[:, hidden:]
    act = gelu_value(pre).astype(jnp.bfloat16)
    pre_grad = (grad * gelu_slope(pre)).astype(jnp.bfloat16)
    mine = jnp.concatenate([act, pre_grad], axis=1)
    mine = lax.all_gather(mine, "zh", axis=0, tiled=True)
    mine = lax.all_gather(mine, "x", axis=0, tiled=True)

    out = jnp.dot(mine[:, :hidden], w_out_all, preferred_element_type=jnp.float32).astype(jnp.bfloat16)
    back = contract_last(mine[:, hidden:], w_in_all).astype(jnp.bfloat16)
    sums = jnp.concatenate([out[:, :features], back[:, :features]], axis=1)
    sums_next = jnp.concatenate([out[:, features:], back[:, features:]], axis=1)
    sums = jnp.concatenate([sums, sums_next], axis=0).reshape(2, 2, 4, 2, -1, 2 * features)
    sums = sums.transpose(0, 1, 3, 2, 4, 5).reshape(-1, 2 * features)
    sums = exchange(sums, ("core", "zb", "yb"))
    sums = jnp.sum(sums.reshape(2, 4, -1, 2 * features).astype(jnp.float32), axis=1)
    sums = to_fourth_root(sums.reshape(-1, 2 * features))
    every = core_order(mine, swap_core(mine), 0)
    w_out_grad = contract_first(every[:, :hidden], cotangent)
    w_in_grad = contract_first(inputs, every[:, hidden:])
    sums, w_out_grad, w_in_grad = lax.optimization_barrier((sums, w_out_grad, w_in_grad))
    sums = jnp.sum(from_fourth_root(exchange(sums, ("za", "ya"))), axis=0)
    return (sums[:, :features], sums[:, features:], w_in_grad, w_out_grad)


def solution(mesh):
    axes = ("x", "zh", "core", "za", "zb", "ya", "yb")
    fine = Mesh(mesh.devices.reshape(4, 4, 2, 2, 2, 4, 2), axes)
    row, col = axes[:3], axes[3:]
    in_specs = (P(None, row), P(None, row), P(row, col), P(col, row))
    out_specs = (P(col, row), P(col, row), P(row, col), P(col, row))
    return jax.shard_map(shards, mesh=fine, in_specs=in_specs, out_specs=out_specs, check_vma=False)
```
